32 devices in a mesh: spot: 8 (over y, x, core), gene: 4 (over z).
Axes of the slice: x: 2, y: 2, z: 4, core: 2. Of those that a mesh axis runs over, the one named last changes fastest.
Arguments:
- counts: int32 [32, 512, 4096], P('spot', None, 'gene'), may hold values from 0 to 56, as said below
- tissue: int32 [32, 512], P('spot'), may hold values from 0 to 1
- tile_ids: int32 [32, 512], P('spot'), may hold values from 0 to 16383, as said below
Outputs:
- statistic: float32 [4096, 4096], P('gene', 'spot')
The draws below stay inside these ranges and needn't reach their ends.
Inputs may be any that keep to these rules, and one draw needn't show every extreme that they name: `counts`: whole numbers of molecules. `tile_ids`: bins of one tile form a rectangle of the grid; tiles are bands of rows crossed with bands of columns.
All inputs are finite; a program needn't handle non-finite values.
Results may differ from the reference program's by a relative error of at most 0.003.
Values may be sent and summed in bfloat16 or wider, within the bound.
A program may use at most 128 MiB of HBM per device.

```python
import jax
import jax.numpy as jnp
from jax import lax

G = 4096
GRID_W = 512
GRID_H = 32
N_GENE = 4


def draw_counts(key, part):
    exponents = jax.random.randint(jax.random.fold_in(key, 1), (G,), 0, 4)
    levels = jnp.left_shift(jnp.ones((G,), jnp.int32), exponents.astype(jnp.int32))
    row_pos = jnp.arange(GRID_H, dtype=jnp.int32)
    row_factor = (2 * GRID_H + 6 * row_pos) // GRID_H
    upper = 1 + levels[None, None, :] * row_factor[:, None, None]
    upper = jnp.broadcast_to(upper, (GRID_H, GRID_W, G))
    drawn = jax.random.randint(jax.random.fold_in(key, 2), (GRID_H, GRID_W, G), 0, upper).astype(jnp.int32)
    return drawn.at[GRID_H - 1, 0, 0].set(56).astype(jnp.int32)


def draw_tissue(key, part):
    row_pos = jnp.arange(GRID_H, dtype=jnp.int32)
    threshold = 4 + 11 * row_pos // (GRID_H - 1)
    rolls = jax.random.randint(jax.random.fold_in(key, 21), (GRID_H, GRID_W), 0, 16).astype(jnp.int32)
    return (rolls < threshold[:, None]).astype(jnp.int32)


def draw_tile_ids(key, part):
    row_flags = (jax.random.randint(jax.random.fold_in(key, 11), (GRID_H,), 0, 12) == 0).astype(jnp.int32)
    col_flags = (jax.random.randint(jax.random.fold_in(key, 12), (GRID_W,), 0, 24) == 0).astype(jnp.int32)
    row_flags = jnp.where(jnp.arange(GRID_H, dtype=jnp.int32) == 0, 0, row_flags).astype(jnp.int32)
    col_flags = jnp.where(jnp.arange(GRID_W, dtype=jnp.int32) == 0, 0, col_flags).astype(jnp.int32)
    row_band = jnp.cumsum(row_flags).astype(jnp.int32)
    col_band = jnp.cumsum(col_flags).astype(jnp.int32)
    return (GRID_H * GRID_W - 1 - (row_band[:, None] * GRID_W + col_band[None, :])).astype(jnp.int32)


def setup_inputs(seed: int = 0) -> dict:
    arg_keys = jax.random.split(jax.random.key(seed), 4)
    return {
        "counts": draw_counts(jax.random.fold_in(arg_keys[3], 71), 0),
        "tissue": draw_tissue(jax.random.fold_in(arg_keys[3], 71), 0),
        "tile_ids": draw_tile_ids(jax.random.fold_in(arg_keys[3], 71), 0),
    }


stencil_taps = [(row_off, col_off, 1.0 / (row_off * row_off + col_off * col_off)) for row_off in range(-2, 3) for col_off in range(-2, 3) if row_off != 0 or col_off != 0]

def reference(counts, tissue, tile_ids):
    grid_rows, grid_cols, gene_total = counts.shape
    in_tissue = tissue.astype(jnp.float32)
    tissue_wide = jnp.pad(in_tissue, 2)
    ids_wide = jnp.pad(tile_ids, 2)
    weight_sq = jnp.zeros((grid_rows, grid_cols), jnp.float32)
    same_list = []
    for row_off, col_off, weight in stencil_taps:
        near_ids = ids_wide[2 + row_off:2 + row_off + grid_rows, 2 + col_off:2 + col_off + grid_cols]
        near_tissue = tissue_wide[2 + row_off:2 + row_off + grid_rows, 2 + col_off:2 + col_off + grid_cols]
        same_tile = (near_ids == tile_ids).astype(jnp.float32)
        weight_sq = weight_sq + weight * weight * same_tile * near_tissue
        same_list.append(same_tile)
    pair_norm = jnp.sum(in_tissue * weight_sq)
    tissue_count = jnp.sum(in_tissue)
    panel_width = gene_total // N_GENE

    def panel_fields(panel_index):
        values = lax.dynamic_slice_in_dim(counts, panel_index * panel_width, panel_width, 2).astype(jnp.float32)
        gene_mean = lax.optimization_barrier(jnp.sum(values * in_tissue[:, :, None], axis=(0, 1))) / tissue_count
        centred = (values - gene_mean) * in_tissue[:, :, None]
        variance = lax.optimization_barrier(jnp.sum(centred * centred, axis=(0, 1))) / tissue_count
        zscores = (centred / jnp.sqrt(variance + 1e-05)).astype(jnp.bfloat16)
        zscore_wide = jnp.pad(zscores, ((2, 2), (2, 2), (0, 0)))
        lagged_sum = jnp.zeros(values.shape, jnp.float32)
        for (row_off, col_off, weight), same_tile in zip(stencil_taps, same_list):
            near_z = zscore_wide[2 + row_off:2 + row_off + grid_rows, 2 + col_off:2 + col_off + grid_cols, :]
            lagged_sum = lagged_sum + weight * same_tile[:, :, None] * near_z.astype(jnp.float32)
        lagged = lagged_sum.astype(jnp.bfloat16)
        return (zscores.reshape(-1, panel_width), lagged.reshape(-1, panel_width))
    all_z, all_lag = lax.map(panel_fields, jnp.arange(N_GENE, dtype=jnp.int32))
    lag_cols = jnp.transpose(all_lag, (1, 0, 2)).reshape(-1, gene_total)
    contract = (((0,), (0,)), ((), ()))

    def panel_rows(z_panel):
        return lax.dot_general(z_panel, lag_cols, contract, preferred_element_type=jnp.float32)
    row_blocks = lax.map(panel_rows, all_z)
    return row_blocks.reshape(gene_total, gene_total) / jnp.sqrt(pair_norm)
```

```python
import jax
import jax.numpy as jnp
from jax import lax
from jax.experimental import pallas as pl
from jax.experimental.pallas import tpu as pltpu
from jax.sharding import PartitionSpec as P

stencil_taps = [
    (row_off, col_off, 1.0 / (row_off * row_off + col_off * col_off))
    for row_off in range(-2, 3)
    for col_off in range(-2, 3)
    if row_off != 0 or col_off != 0
]
contract_bins = (((0,), (0,)), ((), ()))


def padded(cells, sides, width):
    for axis, dim in sides:
        count = lax.axis_size(axis)
        ends = count - 1
        head = lax.slice_in_dim(cells, 0, width, axis=dim)
        tail = lax.slice_in_dim(cells, cells.shape[dim] - width, cells.shape[dim], axis=dim)
        cells = jnp.concatenate(
            [
                lax.ppermute(tail, axis, [(i, (i + 1) % count) for i in range(ends)]),
                cells,
                lax.ppermute(head, axis, [((i + 1) % count, i) for i in range(ends)]),
            ],
            axis=dim,
        )
    return cells


def cross_panel(left, right):
    return lax.dot_general(left, right, contract_bins, preferred_element_type=jnp.float32)


def plain_shards(counts, tissue, tile_ids):
    row_count, col_count, panel_width = counts.shape
    tile_code = tile_ids * 2 + tissue
    code_rims = padded(tile_code, (("spot", 0),), 2)
    code_wide = jnp.pad(code_rims, ((0, 0), (2, 2)))
    tissue_wide = (code_wide % 2).astype(jnp.float32)
    ids_wide = code_wide // 2
    in_tissue = tissue.astype(jnp.float32)
    weight_sq = jnp.zeros((row_count, col_count), jnp.float32)
    same_list = []
    for row_off, col_off, weight in stencil_taps:
        near_ids = ids_wide[
            2 + row_off : 2 + row_off + row_count, 2 + col_off : 2 + col_off + col_count
        ]
        near_tissue = tissue_wide[
            2 + row_off : 2 + row_off + row_count, 2 + col_off : 2 + col_off + col_count
        ]
        same_tile = (near_ids == tile_ids).astype(jnp.float32)
        weight_sq = weight_sq + weight * weight * same_tile * near_tissue
        same_list.append(same_tile)
    pair_local = jnp.sum(in_tissue * weight_sq)
    count_local = jnp.sum(in_tissue)
    values = counts.astype(jnp.float32)
    masked = values * in_tissue[:, :, None]
    first_sums = jnp.sum(masked, axis=(0, 1))
    total_first, tissue_count, pair_norm = lax.psum((first_sums, count_local, pair_local), "spot")
    gene_mean = total_first / tissue_count
    centred = (values - gene_mean) * in_tissue[:, :, None]
    variance = lax.psum(jnp.sum(centred * centred, axis=(0, 1)), "spot") / tissue_count
    zscores = (centred / jnp.sqrt(variance + 1e-05)).astype(jnp.bfloat16)
    zscore_rims = padded(zscores, (("spot", 0),), 2)
    zscore_wide = jnp.pad(zscore_rims, ((0, 0), (2, 2), (0, 0)))
    lagged_sum = jnp.zeros(values.shape, jnp.float32)
    for (row_off, col_off, weight), same_tile in zip(stencil_taps, same_list):
        near_z = zscore_wide[
            2 + row_off : 2 + row_off + row_count, 2 + col_off : 2 + col_off + col_count, :
        ]
        lagged_sum = lagged_sum + weight * same_tile[:, :, None] * near_z.astype(jnp.float32)
    lagged = lagged_sum.astype(jnp.bfloat16)
    bin_count = row_count * col_count
    flat_z = zscores.reshape(bin_count, panel_width)
    flat_lag = lagged.reshape(bin_count, panel_width)
    totals = cross_panel(flat_z, lax.all_gather(flat_lag, "gene", axis=1, tiled=True))
    share = lax.psum_scatter(totals, "spot", scatter_dimension=1, tiled=True)
    return share / jnp.sqrt(pair_norm)


weight_table = [
    [0.0 if dr == 0 and dc == 0 else 40.0 / (dr * dr + dc * dc) for dc in range(3)]
    for dr in range(3)
]

P_IN = [(0, 1), (3, 2)]
P_CROSS = [(1, 2), (2, 1)]
P_OUT = [(1, 0), (2, 3)]


def lag_kernel(row_same, z_ref, mat_ref, lag_ref):
    rows = lag_ref.shape[0]

    @pl.loop(0, rows)
    def _(r):
        acc = jnp.dot(mat_ref[0], z_ref[r + 2], preferred_element_type=jnp.float32)
        for step, mat in ((0, 2), (1, 1), (3, 1), (4, 2)):
            part = jnp.dot(mat_ref[mat], z_ref[r + step], preferred_element_type=jnp.float32)
            acc = acc + row_same[r, step] * part
        lag_ref[r] = (acc * (1.0 / 40.0)).astype(lag_ref.dtype)


def lag_call(row_same, z_wide, mats):
    rows = z_wide.shape[0] - 4
    cols, genes = z_wide.shape[1:]
    tall = mats.shape[1]
    return pl.pallas_call(
        lag_kernel,
        out_shape=jax.ShapeDtypeStruct((rows, tall, genes), jnp.bfloat16),
        in_specs=[
            pl.BlockSpec(memory_space=pltpu.SMEM),
            pl.BlockSpec(memory_space=pltpu.VMEM),
            pl.BlockSpec(memory_space=pltpu.VMEM),
        ],
        out_specs=pl.BlockSpec(memory_space=pltpu.VMEM),
        compiler_params=pltpu.CompilerParams(vmem_limit_bytes=40 * 1024 * 1024),
        cost_estimate=pl.CostEstimate(
            flops=rows * 10 * tall * cols * genes, bytes_accessed=12 * 2**20, transcendentals=0
        ),
    )(row_same, z_wide, mats)


def pair_sum(code_all, rows, cols):
    code_wide = jnp.pad(code_all, 2)
    tissue_wide = (code_wide % 2).astype(jnp.float32)
    ids_wide = code_wide // 2
    ids = code_all // 2
    weight_sq = jnp.zeros((rows, cols), jnp.float32)
    for row_off, col_off, weight in stencil_taps:
        window = (slice(2 + row_off, 2 + row_off + rows), slice(2 + col_off, 2 + col_off + cols))
        same_tile = (ids_wide[window] == ids).astype(jnp.float32)
        weight_sq = weight_sq + weight * weight * same_tile * tissue_wide[window]
    return jnp.sum((code_all % 2).astype(jnp.float32) * weight_sq)


def mirrored_shards(counts, tissue, tile_ids):
    rows, cols, width = counts.shape
    half = width // 2
    spots, genes = lax.axis_size("spot"), lax.axis_size("gene")
    spot, g = lax.axis_index("spot"), lax.axis_index("gene")
    core, chip = spot % 2, spot // 2
    x, y = chip % 2, chip // 2
    low, inner = g < 2, (g == 1) | (g == 2)
    swap = lambda a, bit: lax.ppermute(a, "spot", [(i, i ^ bit) for i in range(spots)])
    along = lambda a, perm: lax.ppermute(a, "gene", perm)
    ordered = lambda flag, a, b, dim: jnp.where(
        flag, jnp.concatenate([a, b], dim), jnp.concatenate([b, a], dim)
    )

    code = tile_ids * 2 + tissue
    raw = (counts * tissue[:, :, None]).astype(jnp.bfloat16)
    kept = lax.dynamic_slice_in_dim(raw, core * half, half, 2)
    given = lax.dynamic_slice_in_dim(raw, (1 - core) * half, half, 2)
    taken = swap(given, 1)
    code_taken = swap(code, 1)
    first = core == 0
    both = ordered(first, kept, taken, 0)
    code_both = ordered(first, code, code_taken, 0)
    tissue_both = (code_both % 2).astype(jnp.float32)
    bins_here = jnp.sum(tissue_both)
    both_f = both.astype(jnp.float32)
    shift = jnp.round(jnp.sum(both_f, axis=(0, 1)) / jnp.maximum(bins_here, 1.0))
    dev_f = both_f - tissue_both[:, :, None] * shift
    dev = dev_f.astype(jnp.bfloat16)

    mid, edge = cols // 2, 16
    part_a = jnp.where(low, dev[:, : mid + edge], dev[:, mid - edge :])
    part_b = jnp.where(low, dev[:, mid + edge :], dev[:, : mid - edge])
    pieces = [part_a[:rows], part_a[rows:]]
    in_a = [along(p, P_IN) for p in pieces]
    cross_a = [along(p, P_CROSS) for p in pieces]
    out_inner = [along(p, P_OUT) for p in cross_a]
    cross_outer = [along(p, P_CROSS) for p in in_a]
    in_b = along(part_b, P_IN)
    out_outer = [along(p, P_OUT) for p in cross_outer]

    steps = spots - 2
    above = lax.ppermute(dev[-2:], "spot", [(i, i + 2) for i in range(steps)])
    below = lax.ppermute(dev[:2], "spot", [(i + 2, i) for i in range(steps)])

    code_all = lax.all_gather(code, "spot", axis=0, tiled=True)
    dev_back = dev.astype(jnp.float32)
    local = jnp.stack(
        [
            jnp.sum(dev_back, axis=(0, 1)),
            jnp.sum(dev_back * dev_back, axis=(0, 1)),
            shift,
            jnp.full((half,), bins_here),
        ]
    )
    every = lax.all_gather(local, "spot", axis=0).reshape(spots // 2, 2, 4, half)
    every = lax.dynamic_index_in_dim(every, core, 1, keepdims=False)
    sum1, sum2, shifts, bins = every[:, 0], every[:, 1], every[:, 2], every[:, 3]
    tissue_count = jnp.sum(bins, axis=0)
    mean = jnp.sum(sum1 + bins * shifts, axis=0) / tissue_count
    gap = mean - shifts
    variance = jnp.sum(sum2 - 2.0 * gap * sum1 + bins * gap * gap, axis=0) / tissue_count
    scale = 1.0 / jnp.sqrt(variance + 1e-05)
    pair_norm = pair_sum(code_all, rows * spots, cols)

    band = 2 * rows
    code_pad = jnp.pad(code_all, ((2, 2), (0, 0)), constant_values=-2)
    code_wide = lax.dynamic_slice_in_dim(code_pad, chip * band, band + 4, 0)
    tissue_wide = (code_wide % 2).astype(jnp.float32)
    gap_pad = jnp.pad(gap, ((1, 1), (0, 0)))
    gap_near = lax.dynamic_slice_in_dim(gap_pad, chip, 3, 0)
    gap_here = gap_near[1]
    gap_rows = jnp.concatenate(
        [
            jnp.broadcast_to(gap_near[k], (count, half))
            for k, count in ((0, 2), (1, band), (2, 2))
        ]
    )
    wide = jnp.concatenate([above, dev, below]).astype(jnp.float32)
    z_wide = (
        (wide - tissue_wide[:, :, None] * gap_rows[:, None, :]) * scale
    ).astype(jnp.bfloat16)

    edge_ids = code_wide[:, 0] // 2
    row_same = jnp.stack(
        [(edge_ids[k : k + band] == edge_ids[2 : 2 + band]).astype(jnp.float32) for k in range(5)], 1
    )
    line = code_all[0] // 2
    col_same = line[:, None] == line[None, :]
    spread = jnp.abs(jnp.arange(cols)[:, None] - jnp.arange(cols)[None, :])
    at = lax.broadcasted_iota(jnp.int32, (mid + edge, cols), 0) + jnp.where(low, mid - edge, 0)
    across = (at >= mid) != (lax.broadcasted_iota(jnp.int32, (mid + edge, cols), 1) >= mid)
    here = (at >= mid) == low
    share = jnp.where(across, 0.5, jnp.where(here, 1.0, 0.0))
    cut = lambda a: jnp.where(low, a[mid - edge :], a[: mid + edge])
    mats = []
    for table in weight_table:
        mat = jnp.zeros((cols, cols), jnp.float32)
        for dc, weight in enumerate(table):
            mat = jnp.where(spread == dc, weight, mat)
        mat = jnp.where(col_same, mat, 0.0)
        mats.append(jnp.concatenate([mat, cut(mat) * share]).astype(jnp.bfloat16))
    lag = lag_call(row_same, z_wide, jnp.stack(mats))
    lag_taken = swap(lag, 1)
    lag_both = ordered(first, lag, lag_taken, 2)
    flat = lambda a: a.reshape(-1, a.shape[-1])
    lag_all, lag_part = flat(lag_both[:, :cols]), flat(lag_both[:, cols:])
    tissue_part = jnp.where(low, tissue_both[:, mid - edge :], tissue_both[:, : mid + edge])
    lag_sum = lambda a, t: cross_panel(a, t.reshape(-1, 1).astype(jnp.bfloat16))
    sum_all, sum_part = lag_sum(lag_all, tissue_both), lag_sum(lag_part, tissue_part)

    panels = lax.all_gather(jnp.stack([gap_here, scale]), "gene", axis=0)
    of_panel = lambda h: lax.dynamic_index_in_dim(panels, h, 0, keepdims=False)

    def settle(product, total, h):
        pair = of_panel(h)
        return (product - total * pair[0]) * pair[1]

    own = settle(cross_panel(lag_all, flat(dev)), sum_all, g)
    near_panel = ordered(low, jnp.concatenate(in_a), in_b, 1)
    near = settle(cross_panel(lag_all, flat(near_panel)), sum_all, g ^ 1)
    near = jnp.where(inner, near, 0.0)
    far_in = jnp.concatenate([jnp.where(inner, p, q) for p, q in zip(cross_a, out_inner)])
    far_out = jnp.concatenate([jnp.where(inner, p, q) for p, q in zip(cross_outer, out_outer)])
    far_in = settle(cross_panel(lag_part, flat(far_in)), sum_part, jnp.where(low, 2, 1))
    far_out = settle(cross_panel(lag_part, flat(far_out)), sum_part, jnp.where(low, 3, 0))

    even = g % 2 == 0
    near_0, near_1 = jnp.where(even, own, near), jnp.where(even, near, own)
    far_0, far_1 = jnp.where(low, far_in, far_out), jnp.where(low, far_out, far_in)
    grid = [
        [jnp.where(low, near_0, far_0), jnp.where(low, near_1, far_1)],
        [jnp.where(low, far_0, near_0), jnp.where(low, far_1, near_1)],
    ]
    narrow = lambda a: a.astype(jnp.bfloat16)
    widen = lambda a: a.astype(jnp.float32)

    def fold(blocks, bits, places):
        pairs = blocks
        send = [narrow(jnp.where(places[0] == 0, pairs[1][k], pairs[0][k])) for k in range(2)]
        keep = [jnp.where(places[0] == 0, pairs[0][k], pairs[1][k]) for k in range(2)]
        keep = [a + widen(swap(b, bits[0])) for a, b in zip(keep, send)]
        send = narrow(jnp.where(places[1] == 0, keep[1], keep[0]))
        return jnp.where(places[1] == 0, keep[0], keep[1]) + widen(swap(send, bits[1]))

    top = fold([[grid[i][j][:half] for j in range(2)] for i in range(2)], (4, 2), (y, x))
    bottom = fold([[grid[j][i][half:] for j in range(2)] for i in range(2)], (2, 4), (x, y))

    places = [(h, c, k) for h in range(genes) for c in range(2) for k in range(genes) if h != k]
    where_is = lambda h, c, k: (2 * h + c) * genes + k
    same_core = [(where_is(h, c, k), where_is(k, c, h)) for h, c, k in places]
    other_core = [(where_is(h, c, k), where_is(k, 1 - c, h)) for h, c, k in places]
    top_n, bottom_n = narrow(top), narrow(bottom)
    got_same = lax.ppermute(jnp.where(first, top_n, bottom_n), ("spot", "gene"), same_core)
    got_other = lax.ppermute(jnp.where(first, bottom_n, top_n), ("spot", "gene"), other_core)
    norm = 1.0 / jnp.sqrt(pair_norm)
    top = (top + widen(jnp.where(first, got_same, got_other)).T) * norm
    bottom = (bottom + widen(jnp.where(first, got_other, got_same)).T) * norm
    return jnp.concatenate([top, bottom])


def solution(mesh):
    placed = (P("spot", None, "gene"), P("spot", None), P("spot", None))
    fits = mesh.shape["gene"] == 4 and mesh.shape["spot"] == 8
    return jax.shard_map(
        mirrored_shards if fits else plain_shards,
        mesh=mesh,
        in_specs=placed,
        out_specs=P("gene", "spot"),
        check_vma=False,
    )
```

```python
import jax
import jax.numpy as jnp
from jax import lax
from jax.experimental import pallas as pl
from jax.experimental.pallas import tpu as pltpu
from jax.sharding import PartitionSpec as P

stencil_taps = [
    (row_off, col_off, 1.0 / (row_off * row_off + col_off * col_off))
    for row_off in range(-2, 3)
    for col_off in range(-2, 3)
    if row_off != 0 or col_off != 0
]
contract_bins = (((0,), (0,)), ((), ()))


def padded(cells, sides, width):
    for axis, dim in sides:
        count = lax.axis_size(axis)
        ends = count - 1
        head = lax.slice_in_dim(cells, 0, width, axis=dim)
        tail = lax.slice_in_dim(cells, cells.shape[dim] - width, cells.shape[dim], axis=dim)
        cells = jnp.concatenate(
            [
                lax.ppermute(tail, axis, [(i, (i + 1) % count) for i in range(ends)]),
                cells,
                lax.ppermute(head, axis, [((i + 1) % count, i) for i in range(ends)]),
            ],
            axis=dim,
        )
    return cells


def cross_panel(left, right):
    return lax.dot_general(left, right, contract_bins, preferred_element_type=jnp.float32)


def plain_shards(counts, tissue, tile_ids):
    row_count, col_count, panel_width = counts.shape
    tile_code = tile_ids * 2 + tissue
    code_rims = padded(tile_code, (("spot", 0),), 2)
    code_wide = jnp.pad(code_rims, ((0, 0), (2, 2)))
    tissue_wide = (code_wide % 2).astype(jnp.float32)
    ids_wide = code_wide // 2
    in_tissue = tissue.astype(jnp.float32)
    weight_sq = jnp.zeros((row_count, col_count), jnp.float32)
    same_list = []
    for row_off, col_off, weight in stencil_taps:
        near_ids = ids_wide[
            2 + row_off : 2 + row_off + row_count, 2 + col_off : 2 + col_off + col_count
        ]
        near_tissue = tissue_wide[
            2 + row_off : 2 + row_off + row_count, 2 + col_off : 2 + col_off + col_count
        ]
        same_tile = (near_ids == tile_ids).astype(jnp.float32)
        weight_sq = weight_sq + weight * weight * same_tile * near_tissue
        same_list.append(same_tile)
    pair_local = jnp.sum(in_tissue * weight_sq)
    count_local = jnp.sum(in_tissue)
    values = counts.astype(jnp.float32)
    masked = values * in_tissue[:, :, None]
    first_sums = jnp.sum(masked, axis=(0, 1))
    total_first, tissue_count, pair_norm = lax.psum((first_sums, count_local, pair_local), "spot")
    gene_mean = total_first / tissue_count
    centred = (values - gene_mean) * in_tissue[:, :, None]
    variance = lax.psum(jnp.sum(centred * centred, axis=(0, 1)), "spot") / tissue_count
    zscores = (centred / jnp.sqrt(variance + 1e-05)).astype(jnp.bfloat16)
    zscore_rims = padded(zscores, (("spot", 0),), 2)
    zscore_wide = jnp.pad(zscore_rims, ((0, 0), (2, 2), (0, 0)))
    lagged_sum = jnp.zeros(values.shape, jnp.float32)
    for (row_off, col_off, weight), same_tile in zip(stencil_taps, same_list):
        near_z = zscore_wide[
            2 + row_off : 2 + row_off + row_count, 2 + col_off : 2 + col_off + col_count, :
        ]
        lagged_sum = lagged_sum + weight * same_tile[:, :, None] * near_z.astype(jnp.float32)
    lagged = lagged_sum.astype(jnp.bfloat16)
    bin_count = row_count * col_count
    flat_z = zscores.reshape(bin_count, panel_width)
    flat_lag = lagged.reshape(bin_count, panel_width)
    totals = cross_panel(flat_z, lax.all_gather(flat_lag, "gene", axis=1, tiled=True))
    share = lax.psum_scatter(totals, "spot", scatter_dimension=1, tiled=True)
    return share / jnp.sqrt(pair_norm)


weight_table = [
    [0.0 if dr == 0 and dc == 0 else 40.0 / (dr * dr + dc * dc) for dc in range(3)]
    for dr in range(3)
]

P_IN = [(0, 1), (3, 2)]
P_CROSS = [(1, 2), (2, 1)]
P_OUT = [(1, 0), (2, 3)]


def lag_kernel(row_same, z_ref, mat_ref, lag_ref):
    rows = lag_ref.shape[0]

    @pl.loop(0, rows)
    def _(r):
        acc = jnp.dot(mat_ref[0], z_ref[r + 2], preferred_element_type=jnp.float32)
        for step, mat in ((0, 2), (1, 1), (3, 1), (4, 2)):
            part = jnp.dot(mat_ref[mat], z_ref[r + step], preferred_element_type=jnp.float32)
            acc = acc + row_same[r, step] * part
        lag_ref[r] = (acc * (1.0 / 40.0)).astype(lag_ref.dtype)


def lag_call(row_same, z_wide, mats):
    rows = z_wide.shape[0] - 4
    cols, genes = z_wide.shape[1:]
    tall = mats.shape[1]
    return pl.pallas_call(
        lag_kernel,
        out_shape=jax.ShapeDtypeStruct((rows, tall, genes), jnp.bfloat16),
        in_specs=[
            pl.BlockSpec(memory_space=pltpu.SMEM),
            pl.BlockSpec(memory_space=pltpu.VMEM),
            pl.BlockSpec(memory_space=pltpu.VMEM),
        ],
        out_specs=pl.BlockSpec(memory_space=pltpu.VMEM),
        compiler_params=pltpu.CompilerParams(vmem_limit_bytes=40 * 1024 * 1024),
        cost_estimate=pl.CostEstimate(
            flops=rows * 10 * tall * cols * genes, bytes_accessed=12 * 2**20, transcendentals=0
        ),
    )(row_same, z_wide, mats)


def pair_sum(code_all, rows, cols):
    code_wide = jnp.pad(code_all, 2)
    tissue_wide = (code_wide % 2).astype(jnp.float32)
    ids_wide = code_wide // 2
    ids = code_all // 2
    weight_sq = jnp.zeros((rows, cols), jnp.float32)
    for row_off, col_off, weight in stencil_taps:
        window = (slice(2 + row_off, 2 + row_off + rows), slice(2 + col_off, 2 + col_off + cols))
        same_tile = (ids_wide[window] == ids).astype(jnp.float32)
        weight_sq = weight_sq + weight * weight * same_tile * tissue_wide[window]
    return jnp.sum((code_all % 2).astype(jnp.float32) * weight_sq)


def mirrored_shards(counts, tissue, tile_ids):
    rows, cols, width = counts.shape
    half = width // 2
    spots, genes = lax.axis_size("spot"), lax.axis_size("gene")
    spot, g = lax.axis_index("spot"), lax.axis_index("gene")
    core, chip = spot % 2, spot // 2
    x, y = chip % 2, chip // 2
    low, inner = g < 2, (g == 1) | (g == 2)
    swap = lambda a, bit: lax.ppermute(a, "spot", [(i, i ^ bit) for i in range(spots)])
    along = lambda a, perm: lax.ppermute(a, "gene", perm)
    ordered = lambda flag, a, b, dim: jnp.where(
        flag, jnp.concatenate([a, b], dim), jnp.concatenate([b, a], dim)
    )

    code = tile_ids * 2 + tissue
    raw = (counts * tissue[:, :, None]).astype(jnp.bfloat16)
    kept = lax.dynamic_slice_in_dim(raw, core * half, half, 2)
    given = lax.dynamic_slice_in_dim(raw, (1 - core) * half, half, 2)
    taken = swap(given, 1)
    code_taken = swap(code, 1)
    first = core == 0
    both = ordered(first, kept, taken, 0)
    code_both = ordered(first, code, code_taken, 0)
    tissue_both = (code_both % 2).astype(jnp.float32)
    bins_here = jnp.sum(tissue_both)
    both_f = both.astype(jnp.float32)
    shift = jnp.round(jnp.sum(both_f, axis=(0, 1)) / jnp.maximum(bins_here, 1.0))
    dev_f = both_f - tissue_both[:, :, None] * shift
    dev = dev_f.astype(jnp.bfloat16)

    mid, edge = cols // 2, 16
    part_a = jnp.where(low, dev[:, : mid + edge], dev[:, mid - edge :])
    part_b = jnp.where(low, dev[:, mid + edge :], dev[:, : mid - edge])

    steps = spots - 2
    above = lax.ppermute(dev[-2:], "spot", [(i, i + 2) for i in range(steps)])
    below = lax.ppermute(dev[:2], "spot", [(i + 2, i) for i in range(steps)])

    code_all = lax.all_gather(code, "spot", axis=0, tiled=True)
    dev_back = dev.astype(jnp.float32)
    local = jnp.stack(
        [
            jnp.sum(dev_back, axis=(0, 1)),
            jnp.sum(dev_back * dev_back, axis=(0, 1)),
            shift,
            jnp.full((half,), bins_here),
        ]
    )
    every = lax.all_gather(local, "spot", axis=0).reshape(spots // 2, 2, 4, half)
    every = lax.dynamic_index_in_dim(every, core, 1, keepdims=False)
    sum1, sum2, shifts, bins = every[:, 0], every[:, 1], every[:, 2], every[:, 3]
    tissue_count = jnp.sum(bins, axis=0)
    mean = jnp.sum(sum1 + bins * shifts, axis=0) / tissue_count
    gap = mean - shifts
    variance = jnp.sum(sum2 - 2.0 * gap * sum1 + bins * gap * gap, axis=0) / tissue_count
    scale = 1.0 / jnp.sqrt(variance + 1e-05)
    panels = lax.all_gather(jnp.stack([lax.dynamic_index_in_dim(gap, chip, 0, keepdims=False), scale]), "gene", axis=0)
    part_a, part_b, panels = lax.optimization_barrier((part_a, part_b, panels))
    pieces = [part_a[:rows], part_a[rows:]]
    in_a = [along(p, P_IN) for p in pieces]
    cross_a = [along(p, P_CROSS) for p in pieces]
    above, below, in_a, cross_a = lax.optimization_barrier((above, below, in_a, cross_a))
    out_inner = [along(p, P_OUT) for p in cross_a]
    cross_outer = [along(p, P_CROSS) for p in in_a]
    in_b = along(part_b, P_IN)
    out_outer = [along(p, P_OUT) for p in cross_outer]
    pair_norm = pair_sum(code_all, rows * spots, cols)

    band = 2 * rows
    code_pad = jnp.pad(code_all, ((2, 2), (0, 0)), constant_values=-2)
    code_wide = lax.dynamic_slice_in_dim(code_pad, chip * band, band + 4, 0)
    tissue_wide = (code_wide % 2).astype(jnp.float32)
    gap_pad = jnp.pad(gap, ((1, 1), (0, 0)))
    gap_near = lax.dynamic_slice_in_dim(gap_pad, chip, 3, 0)
    gap_here = gap_near[1]
    gap_rows = jnp.concatenate(
        [
            jnp.broadcast_to(gap_near[k], (count, half))
            for k, count in ((0, 2), (1, band), (2, 2))
        ]
    )
    wide = jnp.concatenate([above, dev, below]).astype(jnp.float32)
    z_wide = (
        (wide - tissue_wide[:, :, None] * gap_rows[:, None, :]) * scale
    ).astype(jnp.bfloat16)

    edge_ids = code_wide[:, 0] // 2
    row_same = jnp.stack(
        [(edge_ids[k : k + band] == edge_ids[2 : 2 + band]).astype(jnp.float32) for k in range(5)], 1
    )
    line = code_all[0] // 2
    col_same = line[:, None] == line[None, :]
    spread = jnp.abs(jnp.arange(cols)[:, None] - jnp.arange(cols)[None, :])
    at = lax.broadcasted_iota(jnp.int32, (mid + edge, cols), 0) + jnp.where(low, mid - edge, 0)
    across = (at >= mid) != (lax.broadcasted_iota(jnp.int32, (mid + edge, cols), 1) >= mid)
    here = (at >= mid) == low
    share = jnp.where(across, 0.5, jnp.where(here, 1.0, 0.0))
    cut = lambda a: jnp.where(low, a[mid - edge :], a[: mid + edge])
    mats = []
    for table in weight_table:
        mat = jnp.zeros((cols, cols), jnp.float32)
        for dc, weight in enumerate(table):
            mat = jnp.where(spread == dc, weight, mat)
        mat = jnp.where(col_same, mat, 0.0)
        mats.append(jnp.concatenate([mat, cut(mat) * share]).astype(jnp.bfloat16))
    lag = lag_call(row_same, z_wide, jnp.stack(mats))
    lag_taken = swap(lag, 1)
    lag_both = ordered(first, lag, lag_taken, 2)
    flat = lambda a: a.reshape(-1, a.shape[-1])
    lag_all, lag_part = flat(lag_both[:, :cols]), flat(lag_both[:, cols:])
    tissue_part = jnp.where(low, tissue_both[:, mid - edge :], tissue_both[:, : mid + edge])
    lag_sum = lambda a, t: cross_panel(a, t.reshape(-1, 1).astype(jnp.bfloat16))
    sum_all, sum_part = lag_sum(lag_all, tissue_both), lag_sum(lag_part, tissue_part)

    of_panel = lambda h: lax.dynamic_index_in_dim(panels, h, 0, keepdims=False)

    def settle(product, total, h):
        pair = of_panel(h)
        return (product - total * pair[0]) * pair[1]

    own = settle(cross_panel(lag_all, flat(dev)), sum_all, g)
    near_panel = ordered(low, jnp.concatenate(in_a), in_b, 1)
    near = settle(cross_panel(lag_all, flat(near_panel)), sum_all, g ^ 1)
    near = jnp.where(inner, near, 0.0)
    far_in = jnp.concatenate([jnp.where(inner, p, q) for p, q in zip(cross_a, out_inner)])
    far_out = jnp.concatenate([jnp.where(inner, p, q) for p, q in zip(cross_outer, out_outer)])
    far_in = settle(cross_panel(lag_part, flat(far_in)), sum_part, jnp.where(low, 2, 1))
    far_out = settle(cross_panel(lag_part, flat(far_out)), sum_part, jnp.where(low, 3, 0))

    even = g % 2 == 0
    near_0, near_1 = jnp.where(even, own, near), jnp.where(even, near, own)
    far_0, far_1 = jnp.where(low, far_in, far_out), jnp.where(low, far_out, far_in)
    grid = [
        [jnp.where(low, near_0, far_0), jnp.where(low, near_1, far_1)],
        [jnp.where(low, far_0, near_0), jnp.where(low, far_1, near_1)],
    ]
    narrow = lambda a: a.astype(jnp.bfloat16)
    widen = lambda a: a.astype(jnp.float32)

    def fold(blocks, bits, places):
        pairs = blocks
        send = [narrow(jnp.where(places[0] == 0, pairs[1][k], pairs[0][k])) for k in range(2)]
        keep = [jnp.where(places[0] == 0, pairs[0][k], pairs[1][k]) for k in range(2)]
        keep = [a + widen(swap(b, bits[0])) for a, b in zip(keep, send)]
        send = narrow(jnp.where(places[1] == 0, keep[1], keep[0]))
        return jnp.where(places[1] == 0, keep[0], keep[1]) + widen(swap(send, bits[1]))

    top = fold([[grid[i][j][:half] for j in range(2)] for i in range(2)], (4, 2), (y, x))
    bottom = fold([[grid[j][i][half:] for j in range(2)] for i in range(2)], (2, 4), (x, y))

    places = [(h, c, k) for h in range(genes) for c in range(2) for k in range(genes) if h != k]
    where_is = lambda h, c, k: (2 * h + c) * genes + k
    same_core = [(where_is(h, c, k), where_is(k, c, h)) for h, c, k in places]
    other_core = [(where_is(h, c, k), where_is(k, 1 - c, h)) for h, c, k in places]
    top_n, bottom_n = narrow(top), narrow(bottom)
    got_same = lax.ppermute(jnp.where(first, top_n, bottom_n), ("spot", "gene"), same_core)
    got_other = lax.ppermute(jnp.where(first, bottom_n, top_n), ("spot", "gene"), other_core)
    norm = 1.0 / jnp.sqrt(pair_norm)
    top = (top + widen(jnp.where(first, got_same, got_other)).T) * norm
    bottom = (bottom + widen(jnp.where(first, got_other, got_same)).T) * norm
    return jnp.concatenate([top, bottom])


def solution(mesh):
    placed = (P("spot", None, "gene"), P("spot", None), P("spot", None))
    fits = mesh.shape["gene"] == 4 and mesh.shape["spot"] == 8
    return jax.shard_map(
        mirrored_shards if fits else plain_shards,
        mesh=mesh,
        in_specs=placed,
        out_specs=P("gene", "spot"),
        check_vma=False,
    )
```

```python
import jax
import jax.numpy as jnp
from jax import lax
from jax.experimental import pallas as pl
from jax.experimental.pallas import tpu as pltpu
from jax.sharding import PartitionSpec as P

stencil_taps = [
    (row_off, col_off, 1.0 / (row_off * row_off + col_off * col_off))
    for row_off in range(-2, 3)
    for col_off in range(-2, 3)
    if row_off != 0 or col_off != 0
]
contract_bins = (((0,), (0,)), ((), ()))


def padded(cells, sides, width):
    for axis, dim in sides:
        count = lax.axis_size(axis)
        ends = count - 1
        head = lax.slice_in_dim(cells, 0, width, axis=dim)
        tail = lax.slice_in_dim(cells, cells.shape[dim] - width, cells.shape[dim], axis=dim)
        cells = jnp.concatenate(
            [
                lax.ppermute(tail, axis, [(i, (i + 1) % count) for i in range(ends)]),
                cells,
                lax.ppermute(head, axis, [((i + 1) % count, i) for i in range(ends)]),
            ],
            axis=dim,
        )
    return cells


def cross_panel(left, right):
    return lax.dot_general(left, right, contract_bins, preferred_element_type=jnp.float32)


def plain_shards(counts, tissue, tile_ids):
    row_count, col_count, panel_width = counts.shape
    tile_code = tile_ids * 2 + tissue
    code_rims = padded(tile_code, (("spot", 0),), 2)
    code_wide = jnp.pad(code_rims, ((0, 0), (2, 2)))
    tissue_wide = (code_wide % 2).astype(jnp.float32)
    ids_wide = code_wide // 2
    in_tissue = tissue.astype(jnp.float32)
    weight_sq = jnp.zeros((row_count, col_count), jnp.float32)
    same_list = []
    for row_off, col_off, weight in stencil_taps:
        near_ids = ids_wide[
            2 + row_off : 2 + row_off + row_count, 2 + col_off : 2 + col_off + col_count
        ]
        near_tissue = tissue_wide[
            2 + row_off : 2 + row_off + row_count, 2 + col_off : 2 + col_off + col_count
        ]
        same_tile = (near_ids == tile_ids).astype(jnp.float32)
        weight_sq = weight_sq + weight * weight * same_tile * near_tissue
        same_list.append(same_tile)
    pair_local = jnp.sum(in_tissue * weight_sq)
    count_local = jnp.sum(in_tissue)
    values = counts.astype(jnp.float32)
    masked = values * in_tissue[:, :, None]
    first_sums = jnp.sum(masked, axis=(0, 1))
    total_first, tissue_count, pair_norm = lax.psum((first_sums, count_local, pair_local), "spot")
    gene_mean = total_first / tissue_count
    centred = (values - gene_mean) * in_tissue[:, :, None]
    variance = lax.psum(jnp.sum(centred * centred, axis=(0, 1)), "spot") / tissue_count
    zscores = (centred / jnp.sqrt(variance + 1e-05)).astype(jnp.bfloat16)
    zscore_rims = padded(zscores, (("spot", 0),), 2)
    zscore_wide = jnp.pad(zscore_rims, ((0, 0), (2, 2), (0, 0)))
    lagged_sum = jnp.zeros(values.shape, jnp.float32)
    for (row_off, col_off, weight), same_tile in zip(stencil_taps, same_list):
        near_z = zscore_wide[
            2 + row_off : 2 + row_off + row_count, 2 + col_off : 2 + col_off + col_count, :
        ]
        lagged_sum = lagged_sum + weight * same_tile[:, :, None] * near_z.astype(jnp.float32)
    lagged = lagged_sum.astype(jnp.bfloat16)
    bin_count = row_count * col_count
    flat_z = zscores.reshape(bin_count, panel_width)
    flat_lag = lagged.reshape(bin_count, panel_width)
    totals = cross_panel(flat_z, lax.all_gather(flat_lag, "gene", axis=1, tiled=True))
    share = lax.psum_scatter(totals, "spot", scatter_dimension=1, tiled=True)
    return share / jnp.sqrt(pair_norm)


weight_table = [
    [0.0 if dr == 0 and dc == 0 else 40.0 / (dr * dr + dc * dc) for dc in range(3)]
    for dr in range(3)
]

P_IN = [(0, 1), (3, 2)]
P_CROSS = [(1, 2), (2, 1)]
P_OUT = [(1, 0), (2, 3)]


def lag_kernel(row_same, z_ref, mat_ref, lag_ref):
    rows = lag_ref.shape[0]

    @pl.loop(0, rows)
    def _(r):
        acc = jnp.dot(mat_ref[0], z_ref[r + 2], preferred_element_type=jnp.float32)
        for step, mat in ((0, 2), (1, 1), (3, 1), (4, 2)):
            part = jnp.dot(mat_ref[mat], z_ref[r + step], preferred_element_type=jnp.float32)
            acc = acc + row_same[r, step] * part
        lag_ref[r] = (acc * (1.0 / 40.0)).astype(lag_ref.dtype)


def lag_call(row_same, z_wide, mats):
    rows = z_wide.shape[0] - 4
    cols, genes = z_wide.shape[1:]
    tall = mats.shape[1]
    return pl.pallas_call(
        lag_kernel,
        out_shape=jax.ShapeDtypeStruct((rows, tall, genes), jnp.bfloat16),
        in_specs=[
            pl.BlockSpec(memory_space=pltpu.SMEM),
            pl.BlockSpec(memory_space=pltpu.VMEM),
            pl.BlockSpec(memory_space=pltpu.VMEM),
        ],
        out_specs=pl.BlockSpec(memory_space=pltpu.VMEM),
        compiler_params=pltpu.CompilerParams(vmem_limit_bytes=40 * 1024 * 1024),
        cost_estimate=pl.CostEstimate(
            flops=rows * 10 * tall * cols * genes, bytes_accessed=12 * 2**20, transcendentals=0
        ),
    )(row_same, z_wide, mats)


def pair_sum(code_all, rows, cols):
    code_wide = jnp.pad(code_all, 2)
    tissue_wide = (code_wide % 2).astype(jnp.float32)
    ids_wide = code_wide // 2
    ids = code_all // 2
    weight_sq = jnp.zeros((rows, cols), jnp.float32)
    for row_off, col_off, weight in stencil_taps:
        window = (slice(2 + row_off, 2 + row_off + rows), slice(2 + col_off, 2 + col_off + cols))
        same_tile = (ids_wide[window] == ids).astype(jnp.float32)
        weight_sq = weight_sq + weight * weight * same_tile * tissue_wide[window]
    return jnp.sum((code_all % 2).astype(jnp.float32) * weight_sq)


def mirrored_shards(counts, tissue, tile_ids):
    rows, cols, width = counts.shape
    half = width // 2
    spots, genes = lax.axis_size("spot"), lax.axis_size("gene")
    spot, g = lax.axis_index("spot"), lax.axis_index("gene")
    core, chip = spot % 2, spot // 2
    x, y = chip % 2, chip // 2
    low, inner = g < 2, (g == 1) | (g == 2)
    swap = lambda a, bit: lax.ppermute(a, "spot", [(i, i ^ bit) for i in range(spots)])
    along = lambda a, perm: lax.ppermute(a, "gene", perm)
    ordered = lambda flag, a, b, dim: jnp.where(
        flag, jnp.concatenate([a, b], dim), jnp.concatenate([b, a], dim)
    )

    code = tile_ids * 2 + tissue
    raw = (counts * tissue[:, :, None]).astype(jnp.bfloat16)
    kept = lax.dynamic_slice_in_dim(raw, core * half, half, 2)
    given = lax.dynamic_slice_in_dim(raw, (1 - core) * half, half, 2)
    taken = swap(given, 1)
    code_taken = swap(code, 1)
    first = core == 0
    both = ordered(first, kept, taken, 0)
    code_both = ordered(first, code, code_taken, 0)
    tissue_both = (code_both % 2).astype(jnp.float32)
    bins_here = jnp.sum(tissue_both)
    both_f = both.astype(jnp.float32)
    shift = jnp.round(jnp.sum(both_f, axis=(0, 1)) / jnp.maximum(bins_here, 1.0))
    dev_f = both_f - tissue_both[:, :, None] * shift
    dev = dev_f.astype(jnp.bfloat16)

    mid, edge = cols // 2, 16
    part_a = jnp.where(low, dev[:, : mid + edge], dev[:, mid - edge :])
    part_b = jnp.where(low, dev[:, mid + edge :], dev[:, : mid - edge])

    steps = spots - 2
    above = lax.ppermute(dev[-2:], "spot", [(i, i + 2) for i in range(steps)])
    below = lax.ppermute(dev[:2], "spot", [(i + 2, i) for i in range(steps)])

    code_all = lax.all_gather(code, "spot", axis=0, tiled=True)
    dev_back = dev.astype(jnp.float32)
    local = jnp.stack(
        [
            jnp.sum(dev_back, axis=(0, 1)),
            jnp.sum(dev_back * dev_back, axis=(0, 1)),
            shift,
            jnp.full((half,), bins_here),
        ]
    )
    every = lax.all_gather(local, "spot", axis=0).reshape(spots // 2, 2, 4, half)
    every = lax.dynamic_index_in_dim(every, core, 1, keepdims=False)
    sum1, sum2, shifts, bins = every[:, 0], every[:, 1], every[:, 2], every[:, 3]
    tissue_count = jnp.sum(bins, axis=0)
    mean = jnp.sum(sum1 + bins * shifts, axis=0) / tissue_count
    gap = mean - shifts
    variance = jnp.sum(sum2 - 2.0 * gap * sum1 + bins * gap * gap, axis=0) / tissue_count
    scale = 1.0 / jnp.sqrt(variance + 1e-05)
    panels = lax.all_gather(jnp.stack([lax.dynamic_index_in_dim(gap, chip, 0, keepdims=False), scale]), "gene", axis=0)
    part_a, part_b, panels = lax.optimization_barrier((part_a, part_b, panels))
    pieces = [part_a[:rows], part_a[rows:]]
    in_a = [along(p, P_IN) for p in pieces]
    cross_a = [along(p, P_CROSS) for p in pieces]
    above, below, in_a, cross_a = lax.optimization_barrier((above, below, in_a, cross_a))
    out_inner = [along(p, P_OUT) for p in cross_a]
    cross_outer = [along(p, P_CROSS) for p in in_a]
    in_b = along(part_b, P_IN)
    pair_norm = pair_sum(code_all, rows * spots, cols)

    band = 2 * rows
    code_pad = jnp.pad(code_all, ((2, 2), (0, 0)), constant_values=-2)
    code_wide = lax.dynamic_slice_in_dim(code_pad, chip * band, band + 4, 0)
    tissue_wide = (code_wide % 2).astype(jnp.float32)
    gap_pad = jnp.pad(gap, ((1, 1), (0, 0)))
    gap_near = lax.dynamic_slice_in_dim(gap_pad, chip, 3, 0)
    gap_here = gap_near[1]
    gap_rows = jnp.concatenate(
        [
            jnp.broadcast_to(gap_near[k], (count, half))
            for k, count in ((0, 2), (1, band), (2, 2))
        ]
    )
    wide = jnp.concatenate([above, dev, below]).astype(jnp.float32)
    z_wide = (
        (wide - tissue_wide[:, :, None] * gap_rows[:, None, :]) * scale
    ).astype(jnp.bfloat16)

    edge_ids = code_wide[:, 0] // 2
    row_same = jnp.stack(
        [(edge_ids[k : k + band] == edge_ids[2 : 2 + band]).astype(jnp.float32) for k in range(5)], 1
    )
    line = code_all[0] // 2
    col_same = line[:, None] == line[None, :]
    spread = jnp.abs(jnp.arange(cols)[:, None] - jnp.arange(cols)[None, :])
    at = lax.broadcasted_iota(jnp.int32, (mid + edge, cols), 0) + jnp.where(low, mid - edge, 0)
    across = (at >= mid) != (lax.broadcasted_iota(jnp.int32, (mid + edge, cols), 1) >= mid)
    here = (at >= mid) == low
    share = jnp.where(across, 0.5, jnp.where(here, 1.0, 0.0))
    cut = lambda a: jnp.where(low, a[mid - edge :], a[: mid + edge])
    mats = []
    for table in weight_table:
        mat = jnp.zeros((cols, cols), jnp.float32)
        for dc, weight in enumerate(table):
            mat = jnp.where(spread == dc, weight, mat)
        mat = jnp.where(col_same, mat, 0.0)
        mats.append(jnp.concatenate([mat, cut(mat) * share]).astype(jnp.bfloat16))
    lag = lag_call(row_same, z_wide, jnp.stack(mats))
    lag, out_inner[0], cross_outer[0] = lax.optimization_barrier(
        (lag, out_inner[0], cross_outer[0])
    )
    out_outer = [along(p, P_OUT) for p in cross_outer]
    lag_taken = swap(lag, 1)
    lag_both = ordered(first, lag, lag_taken, 2)
    flat = lambda a: a.reshape(-1, a.shape[-1])
    lag_all, lag_part = flat(lag_both[:, :cols]), flat(lag_both[:, cols:])
    tissue_part = jnp.where(low, tissue_both[:, mid - edge :], tissue_both[:, : mid + edge])
    lag_sum = lambda a, t: cross_panel(a, t.reshape(-1, 1).astype(jnp.bfloat16))
    sum_all, sum_part = lag_sum(lag_all, tissue_both), lag_sum(lag_part, tissue_part)

    of_panel = lambda h: lax.dynamic_index_in_dim(panels, h, 0, keepdims=False)

    def settle(product, total, h):
        pair = of_panel(h)
        return (product - total * pair[0]) * pair[1]

    own = settle(cross_panel(lag_all, flat(dev)), sum_all, g)
    near_panel = ordered(low, jnp.concatenate(in_a), in_b, 1)
    near = settle(cross_panel(lag_all, flat(near_panel)), sum_all, g ^ 1)
    near = jnp.where(inner, near, 0.0)
    far_in = jnp.concatenate([jnp.where(inner, p, q) for p, q in zip(cross_a, out_inner)])
    far_out = jnp.concatenate([jnp.where(inner, p, q) for p, q in zip(cross_outer, out_outer)])
    far_in = settle(cross_panel(lag_part, flat(far_in)), sum_part, jnp.where(low, 2, 1))
    far_out = settle(cross_panel(lag_part, flat(far_out)), sum_part, jnp.where(low, 3, 0))

    even = g % 2 == 0
    near_0, near_1 = jnp.where(even, own, near), jnp.where(even, near, own)
    far_0, far_1 = jnp.where(low, far_in, far_out), jnp.where(low, far_out, far_in)
    grid = [
        [jnp.where(low, near_0, far_0), jnp.where(low, near_1, far_1)],
        [jnp.where(low, far_0, near_0), jnp.where(low, far_1, near_1)],
    ]
    narrow = lambda a: a.astype(jnp.bfloat16)
    widen = lambda a: a.astype(jnp.float32)

    def fold(blocks, bits, places):
        pairs = blocks
        send = [narrow(jnp.where(places[0] == 0, pairs[1][k], pairs[0][k])) for k in range(2)]
        keep = [jnp.where(places[0] == 0, pairs[0][k], pairs[1][k]) for k in range(2)]
        keep = [a + widen(swap(b, bits[0])) for a, b in zip(keep, send)]
        send = narrow(jnp.where(places[1] == 0, keep[1], keep[0]))
        return jnp.where(places[1] == 0, keep[0], keep[1]) + widen(swap(send, bits[1]))

    top = fold([[grid[i][j][:half] for j in range(2)] for i in range(2)], (4, 2), (y, x))
    bottom = fold([[grid[j][i][half:] for j in range(2)] for i in range(2)], (2, 4), (x, y))

    places = [(h, c, k) for h in range(genes) for c in range(2) for k in range(genes) if h != k]
    where_is = lambda h, c, k: (2 * h + c) * genes + k
    same_core = [(where_is(h, c, k), where_is(k, c, h)) for h, c, k in places]
    other_core = [(where_is(h, c, k), where_is(k, 1 - c, h)) for h, c, k in places]
    top_n, bottom_n = narrow(top), narrow(bottom)
    got_same = lax.ppermute(jnp.where(first, top_n, bottom_n), ("spot", "gene"), same_core)
    got_other = lax.ppermute(jnp.where(first, bottom_n, top_n), ("spot", "gene"), other_core)
    norm = 1.0 / jnp.sqrt(pair_norm)
    top = (top + widen(jnp.where(first, got_same, got_other)).T) * norm
    bottom = (bottom + widen(jnp.where(first, got_other, got_same)).T) * norm
    return jnp.concatenate([top, bottom])


def solution(mesh):
    placed = (P("spot", None, "gene"), P("spot", None), P("spot", None))
    fits = mesh.shape["gene"] == 4 and mesh.shape["spot"] == 8
    return jax.shard_map(
        mirrored_shards if fits else plain_shards,
        mesh=mesh,
        in_specs=placed,
        out_specs=P("gene", "spot"),
        check_vma=False,
    )
```
